32 devices in a mesh: pitch: 2 (over x), blk: 16 (over z, y, core).
Axes of the slice: x: 2, y: 2, z: 4, core: 2. Of those that a mesh axis runs over, the one named last changes fastest.
Arguments:
- flux: float32 [128, 16, 45, 128], P('pitch', 'blk'), may hold values from -6 to 6
- pitch_inverse: float32 [16, 128, 128], P('blk', 'pitch')
- span_inverse: float32 [16, 128, 128], P('blk')
- store_old: bfloat16 [2, 16, 32, 45, 128], P('pitch', 'blk'), may hold values from -6 to 6
- send_row: int32 [2, 16, 16], P('pitch', 'blk'), may hold values from 0 to 63
- send_owner: int32 [2, 16, 16], P('pitch', 'blk'), may hold values from 0 to 15, as said below
- send_slot: int32 [2, 16, 16], P('pitch', 'blk'), may hold values from 0 to 31, as said below
- send_count: int32 [2, 16], P('pitch', 'blk'), may hold values from 8 to 16, as said below
Outputs:
- smoothed: float32 [128, 16, 45, 128], P('pitch', 'blk')
- storage: float32 [2, 16, 32, 45, 128], P('pitch', 'blk')
The draws below stay inside these ranges and needn't reach their ends.
Inputs may be any that keep to these rules, and one draw needn't show every extreme that they name: Live entries are the first send_count of each list; in every draw some device has all 16 entries live. `send_owner`: among one device's live entries no owner is named more than 2 times; in every pitch group one owner is named 2 times by the live entries of every device. `send_slot`: within one pitch group, the live entries that name one owner carry distinct slots. `send_row`: the index is r = p * 1 + b on the sending device, with p its local pitch cell and b its local axial cell.
All inputs are finite; a program needn't handle non-finite values.
Results may differ from the reference program's by a relative error of at most 0.0003.
Values sent between devices are 32-bit elements; how exact they have to be, the bound alone decides.
A program may use at most 64 MiB of HBM per device.

```python
import jax
import jax.numpy as jnp
from jax import lax

FIELDS = 5
INSTANCES = 9
P_SIZE = 128
S = 128
CAP = 2
B_DEV = 1
PD = 64
NB = 16
ROWS_DEV = 64
LIST = 16
STORE = 32
N_PITCH = 2
N_BLK = 16


def decay_table(key, blocks, length, extent, periodic, weight):
    key_fall, key_rough, key_centre = jax.random.split(key, 3)
    positions = jnp.arange(length)
    distance = jnp.abs(positions[:, None] - positions[None, :])
    if periodic:
        distance = jnp.minimum(distance, length - distance)
    falloff = jax.random.uniform(key_fall, (blocks, 1, 1), minval=0.55, maxval=0.85)
    decay = jnp.exp(jnp.log(falloff) * distance.astype(jnp.float32) / extent)
    rough = jax.random.uniform(key_rough, (blocks, length, length), minval=0.5, maxval=1.5)
    centre = jax.random.uniform(key_centre, (blocks, length, 1), minval=0.35, maxval=0.65)
    diagonal = centre * jnp.eye(length, dtype=jnp.float32)
    return (weight / extent * rough * decay + diagonal).astype(jnp.float32)


def draw_pitch_inverse(key, part):
    return decay_table(jax.random.fold_in(key, 3), N_BLK, P_SIZE, P_SIZE // N_PITCH, True, 0.125)


def draw_span_inverse(key, part):
    return decay_table(jax.random.fold_in(key, 5), N_BLK, S, max(S // 4, 1), False, 0.15)


def interface_plan(key):
    base = jax.random.fold_in(key, 11)
    key_count, key_full, key_busy, key_order, key_turn, key_perm = jax.random.split(base, 6)
    pairs = N_BLK * CAP
    list_len = N_BLK * CAP // 2
    least = list_len // 4
    live_count = jax.random.randint(key_count, (N_PITCH, N_BLK), list_len // 2, list_len + 1)
    full_dev = jax.random.randint(key_full, (N_PITCH, 1), 0, N_BLK)
    live_count = jnp.where(jnp.arange(N_BLK)[None, :] == full_dev, list_len, live_count)
    busy = jax.random.randint(key_busy, (N_PITCH, 1), 0, N_BLK)
    scores = jax.random.randint(key_order, (N_PITCH, N_BLK, pairs), 1, 65536)
    pair_owner = jnp.arange(pairs) // CAP
    scores = jnp.where(pair_owner[None, None, :] == busy[:, :, None], 0, scores)
    scores = scores * pairs + jnp.arange(pairs)[None, None, :]
    ordering = jnp.argsort(scores, axis=-1)[:, :, :list_len]
    turn = jax.random.randint(key_turn, (N_PITCH, N_BLK, 1), 0, least)
    spots = jnp.arange(list_len)[None, None, :]
    source = jnp.where(spots < least, (spots + turn) % least, spots)
    chosen = jnp.take_along_axis(ordering, source, axis=-1)
    owner = chosen // CAP
    matches = (owner[..., None] == jnp.arange(N_BLK)[None, None, None, :]).astype(jnp.int32)
    rank = jnp.sum(jnp.cumsum(matches, axis=2) * matches, axis=-1) - 1

    def one_perm(number):
        return jax.random.permutation(jax.random.fold_in(key_perm, number), pairs)
    perms = jax.vmap(one_perm)(jnp.arange(N_PITCH * N_BLK))
    sender = jnp.arange(N_BLK)[None, :, None]
    group = jnp.arange(N_PITCH)[:, None, None]
    flat_index = (group * N_BLK + owner) * pairs + sender * CAP + rank
    slot = perms.reshape(-1)[flat_index]
    return (live_count.astype(jnp.int32), owner.astype(jnp.int32), slot.astype(jnp.int32))


def draw_send_count(key, part):
    return interface_plan(key)[0]


def draw_send_owner(key, part):
    return interface_plan(key)[1]


def draw_send_slot(key, part):
    return interface_plan(key)[2]


def with_ends(array, rng, smallest, largest):
    longest = array.shape.index(max(array.shape))
    spots = []
    for shift in (0, 1):
        where = [jax.random.randint(jax.random.fold_in(rng, axis), (), 0, length) for axis, length in enumerate(array.shape)]
        where[longest] = (where[longest] + shift) % array.shape[longest]
        spots.append(tuple(where))
    return array.at[spots[0]].set(smallest).at[spots[1]].set(largest)


def levels(stream_key, shape, pieces, low, top_value):
    factor_of, own = 1.0, jax.random.fold_in(stream_key, 6)
    for position, parts in pieces:
        draws = jnp.exp(jax.random.uniform(jax.random.fold_in(own, position), (parts,), jnp.float32, low / len(pieces), top_value / len(pieces)))
        factor_of = factor_of * jnp.repeat(draws, shape[position] // parts).reshape([-1 if axis == position else 1 for axis in range(len(shape))])
    return factor_of


def scatter_about(rng, shape, scale, reach, cuts=(), kind=jnp.bfloat16):
    gain = levels(rng, shape, cuts, -0.22, 0.18) if cuts else 1.0
    values = jax.random.normal(rng, shape, jnp.float32) * scale * gain
    return jnp.minimum(jnp.maximum(values, -reach), reach).astype(kind)


def setup_inputs(seed: int = 0) -> dict:
    seeds = jax.random.split(jax.random.key(seed), 9)
    flux = scatter_about(seeds[0], (P_SIZE, NB, FIELDS * INSTANCES, S), 1.0, 6.0, ((0, 2), (1, 16)), jnp.float32)
    pitch_inverse = draw_pitch_inverse(jax.random.fold_in(seeds[8], 71), 0)
    span_inverse = draw_span_inverse(jax.random.fold_in(seeds[8], 71), 0)
    store_old = scatter_about(seeds[3], (N_PITCH, N_BLK, STORE, FIELDS * INSTANCES, S), 1.0, 6.0, ((0, 2), (1, 16)))
    send_row = with_ends(jax.random.randint(seeds[4], (N_PITCH, N_BLK, LIST), 0, ROWS_DEV), jax.random.fold_in(seeds[4], 1), 0, ROWS_DEV - 1).astype(jnp.int32)
    send_owner = draw_send_owner(jax.random.fold_in(seeds[8], 71), 0)
    send_slot = draw_send_slot(jax.random.fold_in(seeds[8], 71), 0)
    send_count = draw_send_count(jax.random.fold_in(seeds[8], 71), 0)
    return dict(flux=flux, pitch_inverse=pitch_inverse, span_inverse=span_inverse, store_old=store_old, send_row=send_row, send_owner=send_owner, send_slot=send_slot, send_count=send_count)


def reference(flux, pitch_inverse, span_inverse, store_old, send_row, send_owner, send_slot, send_count):
    highest = lax.Precision.HIGHEST
    padded = jnp.pad(flux, ((0, 0), (1, 1), (0, 0), (0, 0)))
    residual = 0.25 * padded[:, 2:] - 0.75 * padded[:, :-2] + 0.5 * flux
    grouped = residual.reshape(P_SIZE, N_BLK, -1)
    pitch_smoothed = jnp.einsum("dpk,kdx->pdx", pitch_inverse, grouped, precision=highest)
    pitch_smoothed = pitch_smoothed.reshape(P_SIZE, N_BLK, B_DEV, FIELDS * INSTANCES, S)
    smoothed = jnp.einsum("pdbqs,dts->pdbqt", pitch_smoothed, span_inverse, precision=highest)
    smoothed = smoothed.reshape(flux.shape)
    line_index = send_row.astype(jnp.int32)
    group_ids = jnp.arange(N_PITCH).astype(jnp.int32)[:, None, None]
    block_ids = jnp.arange(N_BLK).astype(jnp.int32)[None, :, None]
    pitch_at = group_ids * PD + line_index // B_DEV
    axial_at = block_ids * B_DEV + line_index % B_DEV
    line_rows = smoothed[pitch_at, axial_at]
    is_live = jnp.arange(LIST).astype(jnp.int32)[None, None, :] < send_count.astype(jnp.int32)[:, :, None]
    target = (group_ids * N_BLK + send_owner.astype(jnp.int32)) * STORE + send_slot.astype(jnp.int32)
    target = jnp.where(is_live, target, N_PITCH * N_BLK * STORE).astype(jnp.int32)
    storage = store_old.astype(jnp.float32).reshape(-1, FIELDS * INSTANCES, S)
    storage = storage.at[target.reshape(-1)].set(line_rows.reshape(-1, FIELDS * INSTANCES, S), mode="drop")
    return smoothed, storage.reshape(store_old.shape)
```

```python
import functools

import jax
import jax.numpy as jnp
from jax import lax
from jax.experimental import pallas as pl
from jax.experimental.pallas import tpu as pltpu
from jax.sharding import PartitionSpec as P

CAP = 2
MESH = pl.DeviceIdType.MESH
LAG = 2


def split(x):
    high = x.astype(jnp.bfloat16)
    low = (x - high.astype(jnp.float32)).astype(jnp.bfloat16)
    return high, low


def dot(a, b):
    return lax.dot_general(a, b, (((1,), (0,)), ((), ())), preferred_element_type=jnp.float32)


def dot_t(a, b):
    return lax.dot_general(a, b, (((1,), (1,)), ((), ())), preferred_element_type=jnp.float32)


def iota(shape, dim):
    return lax.broadcasted_iota(jnp.int32, shape, dim)


def to_column(row):
    n = row.shape[1]
    eye = iota((n, n), 0) == iota((n, n), 1)
    return jnp.sum(jnp.where(eye, row, 0), axis=1, keepdims=True)


def kernel(
    n_pitch, n_blk, step, group,
    flux, pitch_op, span_op, row_ref, owner_ref, slot_ref, count_ref,
    out, update, mask,
    low, high, gathered, outgoing, arrived, tags_out, tags_in, lhs, span3, pick,
    low_send, low_recv, high_send, high_recv, y_send, y_recv, row_send, row_recv, tag_send, tag_recv,
):
    comps, lines, cells = flux.shape
    pitch_all = pitch_op.shape[1]
    store = update.shape[1]
    steps = comps // step
    groups = steps // group
    slots = CAP * n_blk
    block_rows = arrived.shape[1] // n_blk
    g = lax.axis_index("pitch")
    me = lax.axis_index("blk")
    f32 = jnp.float32

    def blk_at(k):
        return lax.rem(me + k, n_blk)

    def pitch_at(k):
        return lax.rem(g + k, n_pitch)

    barrier = pltpu.get_barrier_semaphore()

    @pl.loop(1, n_blk)
    def _(k):
        pl.semaphore_signal(barrier, inc=1, device_id={"blk": blk_at(k)}, device_id_type=MESH)

    @pl.loop(1, n_pitch)
    def _(k):
        pl.semaphore_signal(barrier, inc=1, device_id={"pitch": pitch_at(k)}, device_id_type=MESH)

    pl.semaphore_wait(barrier, n_blk - 1 + n_pitch - 1)

    def up(i):
        part = pl.ds(i * step, step)
        return pltpu.make_async_remote_copy(
            src_ref=flux.at[part], dst_ref=low.at[part],
            send_sem=low_send.at[i], recv_sem=low_recv.at[i],
            device_id={"blk": jnp.minimum(me + 1, n_blk - 1)}, device_id_type=MESH,
        )

    def down(i):
        part = pl.ds(i * step, step)
        return pltpu.make_async_remote_copy(
            src_ref=flux.at[part], dst_ref=high.at[part],
            send_sem=high_send.at[i], recv_sem=high_recv.at[i],
            device_id={"blk": jnp.maximum(me - 1, 0)}, device_id_type=MESH,
        )

    own_lines = pl.ds(pl.multiple_of(g * lines, lines), lines)

    def across(i, k):
        ref = gathered.at[pl.ds(i * step, step), own_lines]
        return pltpu.make_async_remote_copy(
            src_ref=ref, dst_ref=ref, send_sem=y_send.at[i, k], recv_sem=y_recv.at[i, k],
            device_id={"pitch": pitch_at(k)}, device_id_type=MESH,
        )

    def rows_to(j, k):
        return pltpu.make_async_remote_copy(
            src_ref=outgoing.at[j, pl.ds(pl.multiple_of(blk_at(k) * block_rows, 8), block_rows)],
            dst_ref=arrived.at[j, pl.ds(pl.multiple_of(me * block_rows, 8), block_rows)],
            send_sem=row_send.at[j, k], recv_sem=row_recv.at[j, k],
            device_id={"blk": blk_at(k)}, device_id_type=MESH,
        )

    def tags_to(k):
        return pltpu.make_async_remote_copy(
            src_ref=tags_out, dst_ref=tags_in.at[me],
            send_sem=tag_send.at[k], recv_sem=tag_recv.at[k],
            device_id={"blk": blk_at(k)}, device_id_type=MESH,
        )

    @pl.loop(0, steps)
    def _(i):
        @pl.when(me < n_blk - 1)
        def _():
            up(i).start()

        @pl.when(me > 0)
        def _():
            down(i).start()

    @pl.when(me == 0)
    def _():
        low[...] = jnp.zeros_like(low)

    @pl.when(me == n_blk - 1)
    def _():
        high[...] = jnp.zeros_like(high)

    entries = owner_ref.shape[1]
    owner = owner_ref[...]
    same = (to_column(owner) == owner) & (iota((entries, entries), 0) < iota((entries, entries), 1))
    rank = jnp.sum(same.astype(jnp.int32), axis=0, keepdims=True)
    live = (iota((1, entries), 1) < count_ref[...]) & (rank < CAP)
    target = jnp.where(live, rank * n_blk + owner, -1)
    here = iota((slots, entries), 0) == target
    line = jnp.sum(jnp.where(here, row_ref[...] + 1, 0), axis=1, keepdims=True) - 1
    choose = (iota((slots, lines), 1) == line).astype(f32).astype(jnp.bfloat16)
    there = to_column(target) == iota((entries, 128), 1)
    tag = jnp.sum(jnp.where(there, to_column(slot_ref[...]) + 1, 0), axis=0, keepdims=True) - 1
    tags_out[...] = jnp.broadcast_to(tag, tags_out.shape)
    tags_in[me] = jnp.broadcast_to(tag, tags_out.shape)

    @pl.loop(1, n_blk)
    def _(k):
        tags_to(k).start()

    a_high, a_low = split(pitch_op[...])
    a_high = jnp.concatenate([a_high.astype(f32), dot(choose, a_high)], axis=0).astype(jnp.bfloat16)
    a_low = jnp.concatenate([a_low.astype(f32), dot(choose, a_low)], axis=0).astype(jnp.bfloat16)
    lhs[...] = jnp.concatenate([a_high, a_high, a_low], axis=1)
    b_high, b_low = split(span_op[...])
    span3[...] = jnp.concatenate([b_high, b_low, b_high], axis=1)

    def place(j):
        @pl.loop(1, n_blk)
        def _(k):
            rows_to(j, k).wait_recv()

        both = pick[...]
        for q in range(group * step):
            parts = [
                arrived[j, pl.ds(q * CAP + c, n_blk, stride=block_rows), :] for c in range(CAP)
            ]
            top, rest = split(jnp.concatenate(parts, axis=0))
            update[j * (group * step) + q] = dot(both, jnp.concatenate([top, rest], axis=0))

    @pl.loop(0, steps + LAG)
    def _(i):
        @pl.when(i < steps)
        def _():
            @pl.when(me > 0)
            def _():
                up(i).wait_recv()

            @pl.when(me < n_blk - 1)
            def _():
                down(i).wait_recv()

            part = pl.ds(i * step, step)
            residual = 0.25 * high[part] - 0.75 * low[part] + 0.5 * flux[part]
            r_high, r_low = split(residual.reshape(step * lines, cells))
            y = dot_t(jnp.concatenate([r_high, r_high, r_low], axis=1), span3[...])
            gathered[part, own_lines, :] = y.reshape(step, lines, cells)

            @pl.loop(1, n_pitch)
            def _(k):
                across(i, k).start()

        @pl.when(i >= LAG)
        def _():
            m = i - LAG

            @pl.loop(1, n_pitch)
            def _(k):
                across(m, k).wait_recv()

            j = m // group
            inner = lax.rem(m, group) * step
            y_high, y_low = split(gathered[pl.ds(m * step, step)])
            stacked = jnp.concatenate([y_high, y_low, y_high], axis=1)
            wide = jnp.concatenate([stacked[q] for q in range(step)], axis=1)
            result = dot(lhs[...], wide)
            for q in range(step):
                piece = result[:, q * cells : (q + 1) * cells]
                out[m * step + q] = piece[:lines]
                for c in range(CAP):
                    first = lines + c * n_blk
                    outgoing[j, pl.ds((inner + q) * CAP + c, n_blk, stride=block_rows), :] = piece[
                        first : first + n_blk
                    ]

            @pl.when(lax.rem(m, group) == group - 1)
            def _():
                @pl.loop(1, n_blk)
                def _(k):
                    rows_to(j, k).start()

                own = pl.ds(pl.multiple_of(me * block_rows, 8), block_rows)
                arrived[j, own, :] = outgoing[j, own, :]

                @pl.when(j == 0)
                def _():
                    @pl.loop(1, n_blk)
                    def _(k):
                        tags_to(k).wait_recv()

                    tags = tags_in[:, 0, :]
                    lanes = iota((n_blk, 128), 1)
                    found = [
                        jnp.sum(jnp.where(lanes == c * n_blk + me, tags, 0), axis=1, keepdims=True)
                        for c in range(CAP)
                    ]
                    spots = iota((n_blk, slots), 1)
                    senders = iota((n_blk, slots), 0)
                    tag_of = jnp.zeros((n_blk, slots), jnp.int32)
                    for c in range(CAP):
                        tag_of = jnp.where(spots == senders + c * n_blk, found[c], tag_of)
                    slot_of = jnp.sum(tag_of, axis=0, keepdims=True)
                    hits = (iota((store, slots), 0) == slot_of).astype(f32)
                    pick[...] = jnp.concatenate([hits, hits], axis=1).astype(jnp.bfloat16)
                    mask[...] = jnp.broadcast_to(jnp.sum(hits, axis=1, keepdims=True), mask.shape)

                @pl.when(j >= 1)
                def _():
                    place(j - 1)

    place(groups - 1)

    @pl.loop(0, steps)
    def _(i):
        @pl.when(me < n_blk - 1)
        def _():
            up(i).wait_send()

        @pl.when(me > 0)
        def _():
            down(i).wait_send()

        @pl.loop(1, n_pitch)
        def _(k):
            across(i, k).wait_send()

    @pl.loop(1, n_blk)
    def _(k):
        tags_to(k).wait_send()

        @pl.loop(0, groups)
        def _(j):
            rows_to(j, k).wait_send()


def local(
    n_pitch, n_blk,
    flux, pitch_inverse, span_inverse, store_old, send_row, send_owner, send_slot, send_count,
):
    lines, _, comps, cells = flux.shape
    pitch_all = pitch_inverse.shape[2]
    store = store_old.shape[2]
    step = next(s for s in (5, 4, 3, 2, 1) if comps % s == 0)
    steps = comps // step
    group = next(s for s in (3, 2, 1) if steps % s == 0)
    groups = steps // group
    slots = CAP * n_blk
    block_rows = -(-(CAP * group * step) // 8) * 8
    f32, dma = jnp.float32, pltpu.SemaphoreType.DMA
    vmem = pl.BlockSpec(memory_space=pltpu.VMEM)
    smoothed, update, mask = pl.pallas_call(
        functools.partial(kernel, n_pitch, n_blk, step, group),
        out_shape=(
            jax.ShapeDtypeStruct((comps, lines, cells), f32),
            jax.ShapeDtypeStruct((comps, store, cells), f32),
            jax.ShapeDtypeStruct((store, 128), f32),
        ),
        in_specs=[vmem] * 7,
        out_specs=(vmem,) * 3,
        scratch_shapes=[
            pltpu.VMEM((comps, lines, cells), f32),
            pltpu.VMEM((comps, lines, cells), f32),
            pltpu.VMEM((comps, pitch_all, cells), f32),
            pltpu.VMEM((groups, n_blk * block_rows, cells), f32),
            pltpu.VMEM((groups, n_blk * block_rows, cells), f32),
            pltpu.VMEM((8, 128), jnp.int32),
            pltpu.VMEM((n_blk, 8, 128), jnp.int32),
            pltpu.VMEM((lines + slots, 3 * pitch_all), jnp.bfloat16),
            pltpu.VMEM((cells, 3 * cells), jnp.bfloat16),
            pltpu.VMEM((store, 2 * slots), jnp.bfloat16),
            dma((steps,)),
            dma((steps,)),
            dma((steps,)),
            dma((steps,)),
            dma((steps, n_pitch)),
            dma((steps, n_pitch)),
            dma((groups, n_blk)),
            dma((groups, n_blk)),
            dma((n_blk,)),
            dma((n_blk,)),
        ],
        compiler_params=pltpu.CompilerParams(
            collective_id=0, has_side_effects=True, vmem_limit_bytes=40 * 2**20
        ),
    )(
        jnp.transpose(flux[:, 0], (1, 0, 2)),
        pitch_inverse[0],
        span_inverse[0],
        send_row[0],
        send_owner[0],
        send_slot[0],
        send_count,
    )
    hit = mask[:, :1, None] > 0
    storage = jnp.where(hit, jnp.transpose(update, (1, 0, 2)), store_old[0, 0].astype(f32))
    return jnp.transpose(smoothed, (1, 0, 2))[:, None], storage[None, None]


def solution(mesh):
    return jax.shard_map(
        functools.partial(local, mesh.shape["pitch"], mesh.shape["blk"]),
        mesh=mesh,
        in_specs=(
            P("pitch", "blk", None, None),
            P("blk", "pitch", None),
            P("blk", None, None),
            P("pitch", "blk", None, None, None),
            P("pitch", "blk", None),
            P("pitch", "blk", None),
            P("pitch", "blk", None),
            P("pitch", "blk"),
        ),
        out_specs=(P("pitch", "blk", None, None), P("pitch", "blk", None, None, None)),
        check_vma=False,
    )
```

```python
import functools

import jax
import jax.numpy as jnp
from jax import lax
from jax.experimental import pallas as pl
from jax.experimental.pallas import tpu as pltpu
from jax.sharding import PartitionSpec as P

CAP = 2
MESH = pl.DeviceIdType.MESH
LAG = 3
AHEAD = 2


def split(x):
    high = x.astype(jnp.bfloat16)
    low = (x - high.astype(jnp.float32)).astype(jnp.bfloat16)
    return high, low


def dot(a, b):
    return lax.dot_general(a, b, (((1,), (0,)), ((), ())), preferred_element_type=jnp.float32)


def dot_t(a, b):
    return lax.dot_general(a, b, (((1,), (1,)), ((), ())), preferred_element_type=jnp.float32)


def iota(shape, dim):
    return lax.broadcasted_iota(jnp.int32, shape, dim)


def to_column(row):
    n = row.shape[1]
    eye = iota((n, n), 0) == iota((n, n), 1)
    return jnp.sum(jnp.where(eye, row, 0), axis=1, keepdims=True)


def kernel(
    n_pitch, n_blk, step, group,
    flux_rows, pitch_op, span_op, row_ref, owner_ref, slot_ref, count_ref,
    out, update, mask,
    flux, low, high, gathered, outgoing, arrived, tags_out, tags_in, lhs, span3, pick,
    low_send, low_recv, high_send, high_recv, y_send, y_recv, row_send, row_recv, tag_send, tag_recv,
):
    comps, lines, cells = flux.shape
    pitch_all = pitch_op.shape[1]
    store = update.shape[1]
    steps = comps // step
    groups = steps // group
    slots = CAP * n_blk
    block_rows = arrived.shape[1] // n_blk
    g = lax.axis_index("pitch")
    me = lax.axis_index("blk")
    f32 = jnp.float32

    def blk_at(k):
        return lax.rem(me + k, n_blk)

    def pitch_at(k):
        return lax.rem(g + k, n_pitch)

    barrier = pltpu.get_barrier_semaphore()

    @pl.loop(1, n_blk)
    def _(k):
        pl.semaphore_signal(barrier, inc=1, device_id={"blk": blk_at(k)}, device_id_type=MESH)

    @pl.loop(1, n_pitch)
    def _(k):
        pl.semaphore_signal(barrier, inc=1, device_id={"pitch": pitch_at(k)}, device_id_type=MESH)

    for q in range(comps):
        flux[q] = flux_rows[pl.ds(q, lines, stride=comps), :]

    def up(i):
        part = pl.ds(i * step, step)
        return pltpu.make_async_remote_copy(
            src_ref=flux.at[part], dst_ref=low.at[part],
            send_sem=low_send.at[i], recv_sem=low_recv.at[i],
            device_id={"blk": jnp.minimum(me + 1, n_blk - 1)}, device_id_type=MESH,
        )

    def down(i):
        part = pl.ds(i * step, step)
        return pltpu.make_async_remote_copy(
            src_ref=flux.at[part], dst_ref=high.at[part],
            send_sem=high_send.at[i], recv_sem=high_recv.at[i],
            device_id={"blk": jnp.maximum(me - 1, 0)}, device_id_type=MESH,
        )

    own_lines = pl.ds(pl.multiple_of(g * lines, lines), lines)

    def across(i, k):
        ref = gathered.at[pl.ds(i * step, step), own_lines]
        return pltpu.make_async_remote_copy(
            src_ref=ref, dst_ref=ref, send_sem=y_send.at[k], recv_sem=y_recv.at[i, k],
            device_id={"pitch": pitch_at(k)}, device_id_type=MESH,
        )

    def rows_to(j, k):
        return pltpu.make_async_remote_copy(
            src_ref=outgoing.at[j, pl.ds(pl.multiple_of(blk_at(k) * block_rows, 8), block_rows)],
            dst_ref=arrived.at[j, pl.ds(pl.multiple_of(me * block_rows, 8), block_rows)],
            send_sem=row_send, recv_sem=row_recv.at[j],
            device_id={"blk": blk_at(k)}, device_id_type=MESH,
        )

    def tags_to(k):
        return pltpu.make_async_remote_copy(
            src_ref=tags_out, dst_ref=tags_in.at[me],
            send_sem=tag_send, recv_sem=tag_recv,
            device_id={"blk": blk_at(k)}, device_id_type=MESH,
        )

    @pl.when(me == 0)
    def _():
        low[...] = jnp.zeros_like(low)

    @pl.when(me == n_blk - 1)
    def _():
        high[...] = jnp.zeros_like(high)

    entries = owner_ref.shape[1]
    owner = owner_ref[...]
    same = (to_column(owner) == owner) & (iota((entries, entries), 0) < iota((entries, entries), 1))
    rank = jnp.sum(same.astype(jnp.int32), axis=0, keepdims=True)
    live = (iota((1, entries), 1) < count_ref[...]) & (rank < CAP)
    target = jnp.where(live, rank * n_blk + owner, -1)
    here = iota((slots, entries), 0) == target
    line = jnp.sum(jnp.where(here, row_ref[...] + 1, 0), axis=1, keepdims=True) - 1
    choose = (iota((slots, lines), 1) == line).astype(f32).astype(jnp.bfloat16)
    there = to_column(target) == iota((entries, 128), 1)
    tag = jnp.sum(jnp.where(there, to_column(slot_ref[...]) + 1, 0), axis=0, keepdims=True) - 1
    tags_out[...] = jnp.broadcast_to(tag, tags_out.shape)
    tags_in[me] = jnp.broadcast_to(tag, tags_out.shape)

    a_high, a_low = split(pitch_op[...])
    a_high = jnp.concatenate([a_high.astype(f32), dot(choose, a_high)], axis=0).astype(jnp.bfloat16)
    a_low = jnp.concatenate([a_low.astype(f32), dot(choose, a_low)], axis=0).astype(jnp.bfloat16)
    lhs[...] = jnp.concatenate([a_high, a_high, a_low], axis=1)
    b_high, b_low = split(span_op[...])
    span3[...] = jnp.concatenate([b_high, b_low, b_high], axis=1)

    pl.semaphore_wait(barrier, n_blk - 1 + n_pitch - 1)

    def halo_start(i):
        @pl.when(me < n_blk - 1)
        def _():
            up(i).start()

        @pl.when(me > 0)
        def _():
            down(i).start()

    def halo_sent(i):
        @pl.when(me < n_blk - 1)
        def _():
            up(i).wait_send()

        @pl.when(me > 0)
        def _():
            down(i).wait_send()

    for i in range(min(AHEAD, steps)):
        halo_start(i)

    @pl.loop(1, n_blk)
    def _(k):
        tags_to(k).start()

    def all_rows(j):
        part = pl.ds(0, (n_blk - 1) * block_rows)
        return pltpu.make_async_remote_copy(
            src_ref=outgoing.at[j, part], dst_ref=arrived.at[j, part],
            send_sem=row_send, recv_sem=row_recv.at[j],
            device_id={"blk": blk_at(1)}, device_id_type=MESH,
        )

    def all_tags():
        part = tags_in.at[pl.ds(0, n_blk - 1)]
        return pltpu.make_async_remote_copy(
            src_ref=part, dst_ref=part, send_sem=tag_send, recv_sem=tag_recv,
            device_id={"blk": blk_at(1)}, device_id_type=MESH,
        )

    def place(j):
        all_rows(j).wait_recv()
        both = pick[...]
        for q in range(group * step):
            parts = [
                arrived[j, pl.ds(q * CAP + c, n_blk, stride=block_rows), :] for c in range(CAP)
            ]
            top, rest = split(jnp.concatenate(parts, axis=0))
            update[j * (group * step) + q] = dot(both, jnp.concatenate([top, rest], axis=0))

    @pl.loop(0, steps + LAG)
    def _(i):
        @pl.when(i < steps)
        def _():
            @pl.when(me > 0)
            def _():
                up(i).wait_recv()

            @pl.when(me < n_blk - 1)
            def _():
                down(i).wait_recv()

            halo_sent(i)

            @pl.when(i + AHEAD < steps)
            def _():
                halo_start(i + AHEAD)

            part = pl.ds(i * step, step)
            residual = 0.25 * high[part] - 0.75 * low[part] + 0.5 * flux[part]
            r_high, r_low = split(residual.reshape(step * lines, cells))
            y = dot_t(jnp.concatenate([r_high, r_high, r_low], axis=1), span3[...])
            gathered[part, own_lines, :] = y.reshape(step, lines, cells)

            @pl.loop(1, n_pitch)
            def _(k):
                across(i, k).start()

        @pl.when(i >= LAG)
        def _():
            m = i - LAG

            @pl.loop(1, n_pitch)
            def _(k):
                across(m, k).wait_recv()

            j = m // group
            inner = lax.rem(m, group) * step
            y_high, y_low = split(gathered[pl.ds(m * step, step)])
            stacked = jnp.concatenate([y_high, y_low, y_high], axis=1)
            wide = jnp.concatenate([stacked[q] for q in range(step)], axis=1)
            result = dot(lhs[...], wide)
            for q in range(step):
                piece = result[:, q * cells : (q + 1) * cells]
                out[pl.ds(m * step + q, lines, stride=comps), :] = piece[:lines]
                for c in range(CAP):
                    first = lines + c * n_blk
                    outgoing[j, pl.ds((inner + q) * CAP + c, n_blk, stride=block_rows), :] = piece[
                        first : first + n_blk
                    ]

            @pl.when(lax.rem(m, group) == group - 1)
            def _():
                @pl.loop(1, n_blk)
                def _(k):
                    rows_to(j, k).start()

                own = pl.ds(pl.multiple_of(me * block_rows, 8), block_rows)
                arrived[j, own, :] = outgoing[j, own, :]

                @pl.when(j == 0)
                def _():
                    all_tags().wait_recv()
                    tags = tags_in[:, 0, :]
                    lanes = iota((n_blk, 128), 1)
                    found = [
                        jnp.sum(jnp.where(lanes == c * n_blk + me, tags, 0), axis=1, keepdims=True)
                        for c in range(CAP)
                    ]
                    spots = iota((n_blk, slots), 1)
                    senders = iota((n_blk, slots), 0)
                    tag_of = jnp.zeros((n_blk, slots), jnp.int32)
                    for c in range(CAP):
                        tag_of = jnp.where(spots == senders + c * n_blk, found[c], tag_of)
                    slot_of = jnp.sum(tag_of, axis=0, keepdims=True)
                    hits = (iota((store, slots), 0) == slot_of).astype(f32)
                    pick[...] = jnp.concatenate([hits, hits], axis=1).astype(jnp.bfloat16)
                    mask[...] = jnp.broadcast_to(jnp.sum(hits, axis=1, keepdims=True), mask.shape)

                @pl.when(j >= 1)
                def _():
                    place(j - 1)

    place(groups - 1)

    @pl.loop(1, n_pitch)
    def _(k):
        ref = gathered.at[:, own_lines]
        pltpu.make_async_remote_copy(
            src_ref=ref, dst_ref=ref, send_sem=y_send.at[k], recv_sem=y_recv.at[0, k],
            device_id={"pitch": pitch_at(k)}, device_id_type=MESH,
        ).wait_send()

    all_tags().wait_send()
    part = pl.ds(0, (n_blk - 1) * block_rows)
    pltpu.make_async_remote_copy(
        src_ref=outgoing.at[:, part], dst_ref=arrived.at[:, part],
        send_sem=row_send, recv_sem=row_recv.at[0],
        device_id={"blk": blk_at(1)}, device_id_type=MESH,
    ).wait_send()


def local(
    n_pitch, n_blk,
    flux, pitch_inverse, span_inverse, store_old, send_row, send_owner, send_slot, send_count,
):
    lines, _, comps, cells = flux.shape
    pitch_all = pitch_inverse.shape[2]
    store = store_old.shape[2]
    step = next(s for s in (5, 4, 3, 2, 1) if comps % s == 0)
    steps = comps // step
    group = next(s for s in (3, 2, 1) if steps % s == 0)
    groups = steps // group
    slots = CAP * n_blk
    block_rows = -(-(CAP * group * step) // 8) * 8
    f32, dma = jnp.float32, pltpu.SemaphoreType.DMA
    vmem = pl.BlockSpec(memory_space=pltpu.VMEM)
    smoothed, update, mask = pl.pallas_call(
        functools.partial(kernel, n_pitch, n_blk, step, group),
        out_shape=(
            jax.ShapeDtypeStruct((lines * comps, cells), f32),
            jax.ShapeDtypeStruct((comps, store, cells), f32),
            jax.ShapeDtypeStruct((store, 128), f32),
        ),
        in_specs=[vmem] * 7,
        out_specs=(vmem,) * 3,
        scratch_shapes=[
            pltpu.VMEM((comps, lines, cells), f32),
            pltpu.VMEM((comps, lines, cells), f32),
            pltpu.VMEM((comps, lines, cells), f32),
            pltpu.VMEM((comps, pitch_all, cells), f32),
            pltpu.VMEM((groups, n_blk * block_rows, cells), f32),
            pltpu.VMEM((groups, n_blk * block_rows, cells), f32),
            pltpu.VMEM((8, 128), jnp.int32),
            pltpu.VMEM((n_blk, 8, 128), jnp.int32),
            pltpu.VMEM((lines + slots, 3 * pitch_all), jnp.bfloat16),
            pltpu.VMEM((cells, 3 * cells), jnp.bfloat16),
            pltpu.VMEM((store, 2 * slots), jnp.bfloat16),
            dma((steps,)),
            dma((steps,)),
            dma((steps,)),
            dma((steps,)),
            dma((n_pitch,)),
            dma((steps, n_pitch)),
            dma,
            dma((groups,)),
            dma,
            dma,
        ],
        compiler_params=pltpu.CompilerParams(
            collective_id=0, has_side_effects=True, vmem_limit_bytes=40 * 2**20
        ),
    )(
        flux.reshape(lines * comps, cells),
        pitch_inverse[0],
        span_inverse[0],
        send_row[0],
        send_owner[0],
        send_slot[0],
        send_count,
    )
    hit = mask[:, :1, None] > 0
    storage = jnp.where(hit, jnp.transpose(update, (1, 0, 2)), store_old[0, 0].astype(f32))
    return smoothed.reshape(flux.shape), storage[None, None]


def solution(mesh):
    return jax.shard_map(
        functools.partial(local, mesh.shape["pitch"], mesh.shape["blk"]),
        mesh=mesh,
        in_specs=(
            P("pitch", "blk", None, None),
            P("blk", "pitch", None),
            P("blk", None, None),
            P("pitch", "blk", None, None, None),
            P("pitch", "blk", None),
            P("pitch", "blk", None),
            P("pitch", "blk", None),
            P("pitch", "blk"),
        ),
        out_specs=(P("pitch", "blk", None, None), P("pitch", "blk", None, None, None)),
        check_vma=False,
    )
```
